32 devices in a mesh: grp: 2 (over y), chan: 4 (over x, core), freq: 4 (over z).
Axes of the slice: x: 2, y: 2, z: 4, core: 2. Of those that a mesh axis runs over, the one named last changes fastest.
Arguments:
- phases: float32 [32, 2048, 256], P(('grp', 'freq'), 'chan'), parts along dimension 0, may hold values from -3.140625 to 3.140625
- tile_pairs: int32 [4, 2, 2], P('chan'), may hold values from 0 to 3
- block_offsets: int32 [4, 2], P('chan'), may hold values from 0 to 1, each once within a row
- owners: int32 [4, 2, 1], P('chan'), may hold values from 0 to 3; in each aligned block of 2 rows (0 to 1, 2 to 3, ..., all dimensions but the last counted through in order) at most 2 rows name the same one
Outputs:
- envelopes: float32 [64, 32, 16384], P(('grp', 'chan', 'freq')), parts along dimension 0
The draws below stay inside these ranges and needn't reach their ends.
There are 2 independent parts, one for each index of `grp`. The reference program is written for one: setup_inputs(seed, part) draws one part's arguments, and reference() takes and returns one part's arrays. A program takes and returns all parts, laid end to end along the dimension named above; an argument that names none is the same for every part. Nothing has to cross between parts.
Inputs may be any that keep to these rules, and one draw needn't show every extreme that they name: `block_offsets`: each channel block's 2 entries name every value once. `owners`: among the 2 entries of one channel block, no owner is named more than 2 times, and some block names one owner exactly 2 times.
All inputs are finite; a program needn't handle non-finite values.
Results may differ from the reference program's by a relative error of at most 0.0033.
Values may be sent and summed in bfloat16 or wider, within the bound.
A program may use at most 128 MiB of HBM per device.

```python
import math
import jax
import jax.numpy as jnp
import numpy as np
from jax import lax

F = 16
NFFT = 512
SEG = 256
TILE = 128
TD = 4
CAP = 2
LAGS = 32
CB = 512
CHANNELS = 2048
LIST = 2
SLOTS = 32
N_CHAN = 4
N_FREQ = 4


def set_ends(array, own_key, least, top_value):
    dims = array.shape
    index_at = [jax.random.randint(jax.random.fold_in(own_key, axis), (), 0, dims[axis]) for axis in range(len(dims))]
    array = array.at[tuple(index_at)].set(least)
    longest = dims.index(max(dims))
    index_at[longest] = (index_at[longest] + 1) % dims[longest]
    return array.at[tuple(index_at)].set(top_value)


def shared_out(own_key, own, number, rows, amount, top, most, slope):
    sequence = jax.random.permutation(own_key, amount)
    packed, ordinary = load_shares(amount, rows * top, most, slope, True), load_shares(amount, rows * top, most, slope, False)
    places = jnp.arange(amount)

    def named(tallies, rotation):
        used = int((tallies > 0).sum())
        fixed = max(1, used // 4)
        shifted = fixed + (places - fixed + rotation * (used - fixed)) % max(1, amount - fixed)
        return jnp.zeros((amount,), jnp.int32).at[sequence[jnp.where(places < fixed, places, shifted)]].set(jnp.asarray(tallies, jnp.int32))

    tallies = jnp.where(number % 4 == 0, named(packed, number // 4), named(ordinary, number - number // 4 - 1))
    mixed = jax.random.permutation(jax.random.fold_in(own, 3), amount)
    source_of, receiver = mixed[0:amount // 2 * 2:2], mixed[1:amount // 2 * 2:2]
    margin = jnp.minimum(tallies[source_of] - 1, most - tallies[receiver]) // 2
    margin = jnp.where((source_of == sequence[0]) | (receiver == sequence[0]) | (tallies[receiver] == 0), 0, jnp.maximum(margin, 0))
    shifted = jax.random.randint(jax.random.fold_in(own, 4), (amount // 2,), 0, 1 << 20) % (margin + 1)
    tallies = tallies.at[source_of].add(-shifted).at[receiver].add(shifted)
    labels = jnp.searchsorted(jnp.cumsum(tallies), jnp.arange(rows * top), side="right").astype(jnp.int32)
    table = labels.reshape(top, rows).T
    table = table[jax.random.permutation(jax.random.fold_in(own, 1), rows)]
    rotation = jax.random.randint(jax.random.fold_in(own, 2), (rows, 1), 0, top)
    return jnp.take_along_axis(table, (jnp.arange(top)[None, :] + rotation) % top, axis=1)


def load_shares(amount, total, bound, slope, full):
    weights = [(1 << 20) // math.isqrt(standing ** slope) + 1 for standing in range(1, amount + 1)]
    largest = bound if full else min(bound, max(-(-total // amount), total * weights[0] // sum(weights)))
    least = 1 if total - largest >= amount - 1 else 0
    counts, surplus = [largest] + [least] * (amount - 1), total - largest - least * (amount - 1)
    while surplus > 0:
        movable = [i for i in range(1, amount) if counts[i] < largest] or [i for i in range(1, amount) if counts[i] < bound]
        whole, left = sum([weights[i] for i in movable]), surplus
        for i in movable:
            more = min(bound - counts[i], max(1, left * weights[i] // whole), surplus)
            counts[i] = counts[i] + more
            surplus = surplus - more
    return np.array(counts)


def setup_inputs(seed: int = 0, part: int = 0) -> dict:
    key_list = jax.random.split(jax.random.key(seed), 5)
    part_keys = jax.random.split(jax.random.fold_in(key_list[4], part), 5)
    phases = jnp.clip(jax.random.uniform(part_keys[0], (F, CHANNELS, SEG), jnp.float32, -3.140625, 3.140625), -3.140625, 3.140625)
    tile_pairs = set_ends(jax.random.randint(key_list[1], (N_CHAN, LIST, 2), 0, TD), jax.random.fold_in(key_list[1], 1), 0, TD - 1).astype(jnp.int32)
    block_offsets = jax.vmap(lambda own: jax.random.permutation(own, LIST))(jax.random.split(key_list[2], N_CHAN)).reshape((N_CHAN, LIST)).astype(jnp.int32)
    owners_keys = jax.random.split(jax.random.fold_in(key_list[3], 1), N_CHAN * LIST // LIST)
    owners_turns = jax.random.permutation(jax.random.fold_in(key_list[3], 3), N_CHAN * LIST // LIST)
    owners = jax.vmap(lambda own, number: shared_out(jax.random.fold_in(key_list[3], 2), own, number, LIST, N_FREQ, 1, CAP, 2))(owners_keys, owners_turns).reshape((N_CHAN, LIST, 1))
    return dict(phases=phases, tile_pairs=tile_pairs, block_offsets=block_offsets, owners=owners)


def spectra_of(phases):
    return jnp.concatenate([jnp.cos(phases), jnp.sin(phases)], axis=-1).astype(jnp.bfloat16)


def lag_table():
    bins = jnp.arange(F, dtype=jnp.float32) + 32.0
    lag_index = jnp.arange(LAGS, dtype=jnp.float32) - float(LAGS // 2)
    angles = (2.0 * math.pi / NFFT) * bins[:, None] * lag_index[None, :]
    cosine = jnp.cos(angles)
    sine_part = jnp.sin(angles)
    real_rows = jnp.concatenate([cosine, sine_part], axis=1)
    imag_rows = jnp.concatenate([-sine_part, cosine], axis=1)
    return jnp.stack([real_rows, imag_rows], axis=1)


def slot_entries(owner_row, owner_count):
    list_len = owner_row.shape[0]
    places = jnp.arange(list_len, dtype=jnp.int32)
    same_owner = owner_row[:, None] == owner_row[None, :]
    earlier_mask = places[None, :] < places[:, None]
    earlier = jnp.sum(jnp.where(same_owner & earlier_mask, 1, 0), axis=1).astype(jnp.int32)
    targets = owner_row * CAP + earlier
    slot_ids = jnp.arange(owner_count * CAP, dtype=jnp.int32)
    matched = targets[None, :] == slot_ids[:, None]
    entries = jnp.sum(jnp.where(matched, places[None, :], 0), axis=1).astype(jnp.int32)
    filled = jnp.where(jnp.any(matched, axis=1), 1.0, 0.0).astype(jnp.float32)
    return entries, filled


def reference(phases, tile_pairs, block_offsets, owners):
    spectra = spectra_of(phases)
    swapped = jnp.concatenate([spectra[..., SEG:], -spectra[..., :SEG]], axis=-1)
    lag_rows = lag_table()
    env_scale = 1.0 / (F * SEG)
    within = jnp.arange(TILE, dtype=jnp.int32)

    def one_block(chan_row):
        rows_t = tile_pairs[chan_row, :, 0]
        cols_u = tile_pairs[chan_row, :, 1]
        offsets = block_offsets[chan_row] + 1
        first_rows = chan_row * CB + rows_t * TILE
        other_rows = ((chan_row + offsets) % N_CHAN) * CB + cols_u * TILE
        left_index = (first_rows[:, None] + within[None, :]).astype(jnp.int32)
        right_index = (other_rows[:, None] + within[None, :]).astype(jnp.int32)
        left_rows = spectra[:, left_index].astype(jnp.float32)
        left_swap = swapped[:, left_index].astype(jnp.float32)
        right_rows = spectra[:, right_index].astype(jnp.float32)
        real_part = jnp.einsum('feik,fejk->efij', left_rows, right_rows)
        imag_part = jnp.einsum('feik,fejk->efij', left_swap, right_rows)
        cross_tiles = jnp.stack([real_part, imag_part], axis=2).reshape(LIST, F, 2, TILE * TILE)
        lagged = jnp.einsum('efrx,frl->elx', cross_tiles, lag_rows, precision=lax.Precision.HIGHEST)
        envelope = (lagged[:, :LAGS] ** 2 + lagged[:, LAGS:] ** 2) * env_scale
        entries, filled = slot_entries(owners[chan_row, :, 0], N_FREQ)
        return jnp.take(envelope, entries, axis=0) * filled[:, None, None]

    result = lax.map(one_block, jnp.arange(N_CHAN, dtype=jnp.int32))
    return result.reshape(SLOTS, LAGS, TILE * TILE)
```

```python
import functools
import math

import jax
import jax.numpy as jnp
import numpy as np
from jax import lax
from jax.experimental import pallas as pl
from jax.experimental.pallas import tpu as pltpu
from jax.sharding import PartitionSpec as P

F = 16
NFFT = 512
TILE = 128
CAP = 2
LAGS = 32
ROW_STEP = 32
MESH = pl.DeviceIdType.MESH

SIN_TERMS = (
    0.999999999982969,
    -0.16666666616916945,
    0.008333330977498568,
    -0.00019840861553013607,
    2.752528712920731e-06,
    -2.3889498620743105e-08,
)
COS_TERMS = (
    0.99999999999925,
    -0.4999999999701845,
    0.04166666647312386,
    -0.0013888884175533636,
    2.4801040301795323e-05,
    -2.752468399134539e-07,
    1.9907690634373785e-09,
)


def polynomial(terms, u):
    total = jnp.full_like(u, terms[-1])
    for term in terms[-2::-1]:
        total = total * u + term
    return total


def cos_sin(x):
    half = x * 0.5
    u = half * half
    s = half * polynomial(SIN_TERMS, u)
    c = polynomial(COS_TERMS, u)
    twice = s + s
    return 1.0 - twice * s, twice * c


def lag_table():
    bins = np.arange(F, dtype=np.float64) + 32.0
    lag_index = np.arange(LAGS, dtype=np.float64) - float(LAGS // 2)
    angles = 2.0 * math.pi / NFFT * bins[:, None] * lag_index[None, :]
    cosine, sine = np.cos(angles), np.sin(angles)
    real_rows = np.concatenate([cosine, sine], axis=1)
    imag_rows = np.concatenate([-sine, cosine], axis=1)
    return np.stack([real_rows, imag_rows], axis=1).reshape(2 * F, 2 * LAGS)


def split_table():
    table = lag_table().T
    high = table.astype(np.float32).astype(jnp.bfloat16)
    low = (table - high.astype(np.float64)).astype(np.float32).astype(jnp.bfloat16)
    return np.concatenate([high, low], axis=1)


def gather_kernel(
    loop,
    line,
    pairs_ref,
    offsets_ref,
    phases_ref,
    all_ref,
    want,
    asked,
    spec,
    going,
    coming,
    own,
    want_send,
    want_recv,
    tile_send,
    tile_recv,
    line_send,
    line_recv,
    local_sem,
):
    me = lax.axis_index("chan")
    pos = lax.axis_index("freq")
    freq_local, block_width, seg_count = phases_ref.shape
    steps = want.shape[0]
    list_len = offsets_ref.shape[1]

    def at_chan(delta):
        return {"chan": lax.rem(me + (delta % loop), loop)}

    def at_freq(delta):
        return {"freq": lax.rem(pos + (delta % line), line)}

    chan_deltas = sorted(
        {(sign * (o + 1)) % loop for o in range(steps) for sign in (1, -1)} - {0}
    )
    freq_deltas = sorted({1 % line, -1 % line} - {0})
    barrier = pltpu.get_barrier_semaphore()
    for delta in chan_deltas:
        pl.semaphore_signal(barrier, inc=1, device_id=at_chan(delta), device_id_type=MESH)
    for delta in freq_deltas:
        pl.semaphore_signal(barrier, inc=1, device_id=at_freq(delta), device_id_type=MESH)
    pl.semaphore_wait(barrier, len(chan_deltas) + len(freq_deltas))

    left_tiles = []
    want_copies = []
    for o in range(steps):
        row_tile = jnp.int32(0)
        col_tile = jnp.int32(0)
        for e in range(list_len):
            here = offsets_ref[0, e] == o
            row_tile = row_tile + jnp.where(here, pairs_ref[0, e, 0], 0)
            col_tile = col_tile + jnp.where(here, pairs_ref[0, e, 1], 0)
        left_tiles.append(row_tile)
        want[o] = jnp.full(want.shape[1:], col_tile, jnp.int32)
        copy = pltpu.make_async_remote_copy(
            src_ref=want.at[o],
            dst_ref=asked.at[o],
            send_sem=want_send.at[o],
            recv_sem=want_recv.at[o],
            device_id=at_chan(o + 1),
            device_id_type=MESH,
        )
        copy.start()
        want_copies.append(copy)

    def tile_of(f, index):
        chosen = spec[f, 0:TILE, :]
        for t in range(1, block_width // TILE):
            chosen = jnp.where(index == t, spec[f, t * TILE : (t + 1) * TILE, :], chosen)
        return chosen

    tile_copies = {}
    asked_tiles = []
    for f in range(freq_local):

        @pl.loop(0, block_width // ROW_STEP)
        def _(step):
            rows = pl.ds(pl.multiple_of(step * ROW_STEP, ROW_STEP), ROW_STEP)
            c, s = cos_sin(phases_ref[f, rows, :])
            spec[f, rows, 0:seg_count] = c.astype(jnp.bfloat16)
            spec[f, rows, seg_count:] = s.astype(jnp.bfloat16)

        if f == 0:
            for o in range(steps):
                want_copies[o].wait_recv()
                asked_tiles.append(jnp.max(asked[o]))
        for o in range(steps):
            going[o, f] = tile_of(f, asked_tiles[o])
            copy = pltpu.make_async_remote_copy(
                src_ref=going.at[o, f],
                dst_ref=coming.at[o, f],
                send_sem=tile_send.at[o, f],
                recv_sem=tile_recv.at[o, f],
                device_id=at_chan(-(o + 1)),
                device_id_type=MESH,
            )
            copy.start()
            tile_copies[o, f] = copy

    units = [(o, f) for f in range(freq_local) for o in range(steps)]

    def line_copy(right, stage, unit, origin, source=None):
        o, f = units[unit]
        place = all_ref.at[o, origin, f]
        way = 0 if right else 1
        return pltpu.make_async_remote_copy(
            src_ref=place if source is None else source,
            dst_ref=place,
            send_sem=line_send.at[way, stage, unit],
            recv_sem=line_recv.at[way, stage, unit],
            device_id=at_freq(1 if right else -1),
            device_id_type=MESH,
        )

    def can_send(right):
        return pos < line - 1 if right else pos > 0

    def arrives(right, stage):
        return pos - (stage + 1) >= 0 if right else pos + (stage + 1) <= line - 1

    def origin_at(right, stage):
        return pos - stage if right else pos + stage

    def take_and_forward(stage, unit):
        for right in (True, False):

            @pl.when(arrives(right, stage))
            def _():
                origin = origin_at(right, stage + 1)
                line_copy(right, stage, unit, origin).wait_recv()
                if stage + 1 < line - 1:

                    @pl.when(can_send(right))
                    def _():
                        line_copy(right, stage + 1, unit, origin).start()

    local_copies = []
    for turn in range(len(units) + line - 1):
        if turn < len(units):
            o, f = units[turn]
            tile_copies[o, f].wait_recv()
            left = tile_of(f, left_tiles[o])
            swapped = jnp.concatenate(
                [left[:, seg_count:], -left[:, :seg_count]], axis=1
            )
            products = lax.dot_general(
                jnp.concatenate([left, swapped], axis=0),
                coming[o, f],
                (((1,), (1,)), ((), ())),
                preferred_element_type=jnp.float32,
            )
            own[o, f, 0] = products[:TILE].astype(own.dtype)
            own[o, f, 1] = products[TILE:].astype(own.dtype)
            for right in (True, False):

                @pl.when(can_send(right))
                def _():
                    line_copy(right, 0, turn, pos, own.at[o, f]).start()

            copy = pltpu.make_async_copy(
                own.at[o, f], all_ref.at[o, pos, f], local_sem.at[turn]
            )
            copy.start()
            local_copies.append(copy)
        for stage in range(line - 1):
            unit = turn - 1 - stage
            if 0 <= unit < len(units):
                take_and_forward(stage, unit)

    for copy in local_copies:
        copy.wait()
    for copy in want_copies:
        copy.wait_send()
    for copy in tile_copies.values():
        copy.wait_send()
    for unit, (o, f) in enumerate(units):
        for right in (True, False):

            @pl.when(can_send(right))
            def _():
                line_copy(right, 0, unit, pos, own.at[o, f]).wait_send()
                for stage in range(line - 2):

                    @pl.when(arrives(right, stage))
                    def _():
                        origin = origin_at(right, stage + 1)
                        line_copy(right, stage + 1, unit, origin).wait_send()


def slot_of(slot, owners_ref, offsets_ref, place_ref):
    earlier, chosen, found = jnp.int32(0), jnp.int32(0), jnp.int32(0)
    for e in range(offsets_ref.shape[0]):
        mine = owners_ref[e] == place_ref[0]
        hit = jnp.logical_and(mine, earlier == slot)
        chosen = jnp.where(hit, offsets_ref[e], chosen)
        found = jnp.where(hit, 1, found)
        earlier = earlier + jnp.where(mine, 1, 0)
    return chosen, found


def lag_kernel(
    env_scale, owners_ref, offsets_ref, place_ref, table_ref, cross_ref, out_ref, by_row
):
    _, parts, rows, width = cross_ref.shape
    _, found = slot_of(pl.program_id(0), owners_ref, offsets_ref, place_ref)
    scale = jnp.where(found == 1, jnp.float32(env_scale), jnp.float32(0.0))
    for k in range(parts):
        by_row[pl.ds(k, rows, stride=parts), :] = cross_ref[0, k].astype(jnp.float32)
    table = table_ref[...]
    for i in range(0, rows, 2):
        pair = jnp.concatenate(
            [
                by_row[pl.ds(i * parts, parts), :],
                by_row[pl.ds((i + 1) * parts, parts), :],
            ],
            axis=1,
        ).astype(jnp.bfloat16)
        lagged = jnp.dot(
            table,
            jnp.concatenate([pair, pair], axis=0),
            preferred_element_type=jnp.float32,
        )
        real, imag = lagged[:LAGS], lagged[LAGS:]
        out_ref[0, :, pl.ds(i * width, 2 * width)] = (real * real + imag * imag) * scale


def on_device(loop, line, phases, tile_pairs, block_offsets, owners):
    freq_local, block_width, seg_count = phases.shape
    steps = loop // 2
    units = steps * freq_local
    list_len = block_offsets.shape[1]
    parts = line * freq_local * 2
    both = 2 * seg_count
    gathered = pl.pallas_call(
        functools.partial(gather_kernel, loop, line),
        out_shape=jax.ShapeDtypeStruct(
            (steps, line, freq_local, 2, TILE, TILE), jnp.bfloat16
        ),
        in_specs=[
            pl.BlockSpec(memory_space=pltpu.SMEM),
            pl.BlockSpec(memory_space=pltpu.SMEM),
            pl.BlockSpec(memory_space=pltpu.VMEM),
        ],
        out_specs=pl.BlockSpec(memory_space=pl.ANY),
        scratch_shapes=[
            pltpu.VMEM((steps, 8, 128), jnp.int32),
            pltpu.VMEM((steps, 8, 128), jnp.int32),
            pltpu.VMEM((freq_local, block_width, both), jnp.bfloat16),
            pltpu.VMEM((steps, freq_local, TILE, both), jnp.bfloat16),
            pltpu.VMEM((steps, freq_local, TILE, both), jnp.bfloat16),
            pltpu.VMEM((steps, freq_local, 2, TILE, TILE), jnp.bfloat16),
            pltpu.SemaphoreType.DMA((steps,)),
            pltpu.SemaphoreType.DMA((steps,)),
            pltpu.SemaphoreType.DMA((steps, freq_local)),
            pltpu.SemaphoreType.DMA((steps, freq_local)),
            pltpu.SemaphoreType.DMA((2, line - 1, units)),
            pltpu.SemaphoreType.DMA((2, line - 1, units)),
            pltpu.SemaphoreType.DMA((units,)),
        ],
        compiler_params=pltpu.CompilerParams(
            collective_id=0, has_side_effects=True, vmem_limit_bytes=32 * 2**20
        ),
        name="gather_products",
    )(tile_pairs, block_offsets, phases)

    rows = 32
    place = lax.axis_index("freq").astype(jnp.int32).reshape(1)

    def cross_block(slot, part, *refs):
        return slot_of(slot, *refs)[0], 0, part, 0

    return pl.pallas_call(
        functools.partial(lag_kernel, 1.0 / (F * seg_count)),
        out_shape=jax.ShapeDtypeStruct((CAP, LAGS, TILE * TILE), jnp.float32),
        grid_spec=pltpu.PrefetchScalarGridSpec(
            num_scalar_prefetch=3,
            grid=(CAP, TILE // rows),
            in_specs=[
                pl.BlockSpec((2 * LAGS, 2 * parts), lambda *_: (0, 0)),
                pl.BlockSpec((1, parts, rows, TILE), cross_block),
            ],
            out_specs=pl.BlockSpec(
                (1, LAGS, rows * TILE), lambda slot, part, *_: (slot, 0, part)
            ),
            scratch_shapes=[pltpu.VMEM((rows * parts, TILE), jnp.float32)],
        ),
        compiler_params=pltpu.CompilerParams(vmem_limit_bytes=24 * 2**20),
        name="lag_sums",
    )(
        owners.reshape(list_len),
        block_offsets.reshape(list_len),
        place,
        jnp.asarray(split_table()),
        gathered.reshape(steps, parts, TILE, TILE),
    )


def solution(mesh):
    in_specs = (
        P(("grp", "freq"), "chan", None),
        P("chan", None, None),
        P("chan", None),
        P("chan", None, None),
    )
    out_specs = P(("grp", "chan", "freq"), None, None)
    return jax.shard_map(
        functools.partial(on_device, mesh.shape["chan"], mesh.shape["freq"]),
        mesh=mesh,
        in_specs=in_specs,
        out_specs=out_specs,
        check_vma=False,
    )
```

```python
import functools
import math

import jax
import jax.numpy as jnp
import numpy as np
from jax import lax
from jax.experimental import pallas as pl
from jax.experimental.pallas import tpu as pltpu
from jax.sharding import PartitionSpec as P

F = 16
NFFT = 512
TILE = 128
CAP = 2
LAGS = 32
ROW_STEP = 32
SUBLANES = 16
MESH = pl.DeviceIdType.MESH

SIN_TERMS = (
    0.999999999982969,
    -0.16666666616916945,
    0.008333330977498568,
    -0.00019840861553013607,
    2.752528712920731e-06,
    -2.3889498620743105e-08,
)
COS_TERMS = (
    0.99999999999925,
    -0.4999999999701845,
    0.04166666647312386,
    -0.0013888884175533636,
    2.4801040301795323e-05,
    -2.752468399134539e-07,
    1.9907690634373785e-09,
)


def polynomial(terms, u):
    total = jnp.full_like(u, terms[-1])
    for term in terms[-2::-1]:
        total = total * u + term
    return total


def cos_sin(x):
    half = x * 0.5
    u = half * half
    s = half * polynomial(SIN_TERMS, u)
    c = polynomial(COS_TERMS, u)
    twice = s + s
    return 1.0 - twice * s, twice * c


def lag_table():
    bins = np.arange(F, dtype=np.float64) + 32.0
    lag_index = np.arange(LAGS, dtype=np.float64) - float(LAGS // 2)
    angles = 2.0 * math.pi / NFFT * bins[:, None] * lag_index[None, :]
    cosine, sine = np.cos(angles), np.sin(angles)
    real_rows = np.concatenate([cosine, sine], axis=1)
    imag_rows = np.concatenate([-sine, cosine], axis=1)
    return np.stack([real_rows, imag_rows], axis=1).reshape(2 * F, 2 * LAGS)


def row_table(parts, rows):
    table = lag_table().reshape(2 * F // parts, parts, 2 * LAGS)
    spread = np.einsum("ab,ukl->alubk", np.eye(rows), table)
    spread = spread.reshape(rows * 2 * LAGS, 2 * F * rows)
    high = spread.astype(np.float32).astype(jnp.bfloat16)
    low = (spread - high.astype(np.float64)).astype(np.float32).astype(jnp.bfloat16)
    return np.concatenate([high, low], axis=1)


def gather_kernel(
    loop,
    line,
    group,
    halves,
    pairs_hbm,
    offsets_hbm,
    phases_hbm,
    all_ref,
    pairs_ref,
    offsets_ref,
    phases_ref,
    want,
    asked,
    spec,
    going,
    coming,
    mixed,
    own,
    in_sem,
    want_send,
    want_recv,
    tile_send,
    tile_recv,
    line_send,
    line_recv,
    local_sem,
):
    me = lax.axis_index("chan")
    pos = lax.axis_index("freq")
    freq_local, block_width, seg_count = phases_ref.shape
    steps = want.shape[0]
    list_len = offsets_ref.shape[1]

    sources = [(pairs_hbm, pairs_ref), (offsets_hbm, offsets_ref)]
    sources += [(phases_hbm.at[f], phases_ref.at[f]) for f in range(freq_local)]
    fetched = [
        pltpu.make_async_copy(source, target, in_sem.at[n])
        for n, (source, target) in enumerate(sources)
    ]
    for copy in fetched:
        copy.start()

    def at_chan(delta):
        return {"chan": lax.rem(me + (delta % loop), loop)}

    def at_freq(delta):
        return {"freq": lax.rem(pos + (delta % line), line)}

    chan_deltas = sorted(
        {(sign * (o + 1)) % loop for o in range(steps) for sign in (1, -1)} - {0}
    )
    freq_deltas = sorted({1 % line, -1 % line} - {0})
    barrier = pltpu.get_barrier_semaphore()
    for delta in chan_deltas:
        pl.semaphore_signal(barrier, inc=1, device_id=at_chan(delta), device_id_type=MESH)
    for delta in freq_deltas:
        pl.semaphore_signal(barrier, inc=1, device_id=at_freq(delta), device_id_type=MESH)
    pl.semaphore_wait(barrier, len(chan_deltas) + len(freq_deltas))

    fetched[0].wait()
    fetched[1].wait()

    left_tiles = []
    want_copies = []
    for o in range(steps):
        row_tile = jnp.int32(0)
        col_tile = jnp.int32(0)
        for e in range(list_len):
            here = offsets_ref[0, e] == o
            row_tile = row_tile + jnp.where(here, pairs_ref[0, e, 0], 0)
            col_tile = col_tile + jnp.where(here, pairs_ref[0, e, 1], 0)
        left_tiles.append(row_tile)
        want[o] = jnp.full(want.shape[1:], col_tile, jnp.int32)
        copy = pltpu.make_async_remote_copy(
            src_ref=want.at[o],
            dst_ref=asked.at[o],
            send_sem=want_send.at[o],
            recv_sem=want_recv.at[o],
            device_id=at_chan(o + 1),
            device_id_type=MESH,
        )
        copy.start()
        want_copies.append(copy)

    def tile_of(f, index):
        chosen = spec[f, 0:TILE, :]
        for t in range(1, block_width // TILE):
            chosen = jnp.where(index == t, spec[f, t * TILE : (t + 1) * TILE, :], chosen)
        return chosen

    tile_copies = {}
    asked_tiles = []
    for g in range(freq_local // group):
        for f in range(g * group, (g + 1) * group):
            fetched[2 + f].wait()

            @pl.loop(0, block_width // ROW_STEP)
            def _(step):
                rows = pl.ds(pl.multiple_of(step * ROW_STEP, ROW_STEP), ROW_STEP)
                c, s = cos_sin(phases_ref[f, rows, :])
                spec[f, rows, 0:seg_count] = c.astype(jnp.bfloat16)
                spec[f, rows, seg_count:] = s.astype(jnp.bfloat16)

        for o in range(steps):
            if g == 0:
                want_copies[o].wait_recv()
                asked_tiles.append(jnp.max(asked[o]))
            for f in range(g * group, (g + 1) * group):
                going[o, f] = tile_of(f, asked_tiles[o])
                copy = pltpu.make_async_remote_copy(
                    src_ref=going.at[o, f],
                    dst_ref=coming.at[o, f],
                    send_sem=tile_send.at[o, f],
                    recv_sem=tile_recv.at[o, f],
                    device_id=at_chan(-(o + 1)),
                    device_id_type=MESH,
                )
                copy.start()
                tile_copies[o, f] = copy

    units = [
        (o, g, h)
        for g in range(freq_local // group)
        for o in range(steps)
        for h in range(halves)
    ]
    part_rows = TILE * 2 * group // halves

    def line_copy(right, stage, unit, origin, source=None):
        o, g, h = units[unit]
        place = all_ref.at[o, origin, g, h]
        way = 0 if right else 1
        return pltpu.make_async_remote_copy(
            src_ref=place if source is None else source,
            dst_ref=place,
            send_sem=line_send.at[way, stage, unit],
            recv_sem=line_recv.at[way, stage, unit],
            device_id=at_freq(1 if right else -1),
            device_id_type=MESH,
        )

    def can_send(right):
        return pos < line - 1 if right else pos > 0

    def arrives(right, stage):
        return pos - (stage + 1) >= 0 if right else pos + (stage + 1) <= line - 1

    def origin_at(right, stage):
        return pos - stage if right else pos + stage

    def take_and_forward(stage, unit):
        for right in (True, False):

            @pl.when(arrives(right, stage))
            def _():
                origin = origin_at(right, stage + 1)
                line_copy(right, stage, unit, origin).wait_recv()
                if stage + 1 < line - 1:

                    @pl.when(can_send(right))
                    def _():
                        line_copy(right, stage + 1, unit, origin).start()

    local_copies = []
    for turn in range(len(units) + line - 1):
        if turn < len(units):
            o, g, h = units[turn]
            if h == 0:
                for n in range(group):
                    f = g * group + n
                    tile_copies[o, f].wait_recv()
                    left = tile_of(f, left_tiles[o])
                    swapped = jnp.concatenate(
                        [left[:, seg_count:], -left[:, :seg_count]], axis=1
                    )
                    products = lax.dot_general(
                        jnp.concatenate([left, swapped], axis=0),
                        coming[o, f],
                        (((1,), (1,)), ((), ())),
                        preferred_element_type=jnp.float32,
                    )
                    stride = 2 * group
                    mixed[pl.ds(2 * n, TILE, stride=stride), :] = products[:TILE]
                    mixed[pl.ds(2 * n + 1, TILE, stride=stride), :] = products[TILE:]
            own[o, g, h] = mixed[h * part_rows : (h + 1) * part_rows, :].astype(own.dtype)
            for right in (True, False):

                @pl.when(can_send(right))
                def _():
                    line_copy(right, 0, turn, pos, own.at[o, g, h]).start()

            copy = pltpu.make_async_copy(
                own.at[o, g, h], all_ref.at[o, pos, g, h], local_sem.at[turn]
            )
            copy.start()
            local_copies.append(copy)
        for stage in range(line - 1):
            unit = turn - 1 - stage
            if 0 <= unit < len(units):
                take_and_forward(stage, unit)

    for copy in local_copies:
        copy.wait()
    for copy in want_copies:
        copy.wait_send()
    for copy in tile_copies.values():
        copy.wait_send()
    for unit, (o, g, h) in enumerate(units):
        for right in (True, False):

            @pl.when(can_send(right))
            def _():
                line_copy(right, 0, unit, pos, own.at[o, g, h]).wait_send()
                for stage in range(line - 2):

                    @pl.when(arrives(right, stage))
                    def _():
                        origin = origin_at(right, stage + 1)
                        line_copy(right, stage + 1, unit, origin).wait_send()


def slot_of(slot, owners_ref, offsets_ref, place_ref):
    earlier, chosen, found = jnp.int32(0), jnp.int32(0), jnp.int32(0)
    for e in range(offsets_ref.shape[0]):
        mine = owners_ref[e] == place_ref[0]
        hit = jnp.logical_and(mine, earlier == slot)
        chosen = jnp.where(hit, offsets_ref[e], chosen)
        found = jnp.where(hit, 1, found)
        earlier = earlier + jnp.where(mine, 1, 0)
    return chosen, found


def lag_kernel(
    env_scale, owners_ref, offsets_ref, place_ref, table_ref, cross_ref, out_ref
):
    _, groups, block_rows, width = cross_ref.shape
    _, found = slot_of(pl.program_id(0), owners_ref, offsets_ref, place_ref)
    scale = jnp.where(found == 1, jnp.float32(env_scale), jnp.float32(0.0))
    table = table_ref[...]
    rows_at_once = table.shape[0] // (2 * LAGS)

    def stacked(at):
        start = at * SUBLANES
        return jnp.concatenate(
            [cross_ref[0, u, start : start + SUBLANES, :] for u in range(groups)], axis=0
        )

    for at in range(0, block_rows // SUBLANES, 2):
        pair = jnp.concatenate([stacked(at), stacked(at + 1)], axis=1)
        lagged = jnp.dot(
            table,
            jnp.concatenate([pair, pair], axis=0),
            preferred_element_type=jnp.float32,
        )
        for i in range(rows_at_once):
            start = i * 2 * LAGS
            real = lagged[start : start + LAGS]
            imag = lagged[start + LAGS : start + 2 * LAGS]
            envelope = (real * real + imag * imag) * scale
            for n in range(2):
                place = ((at + n) * rows_at_once + i) * width
                out_ref[0, :, place : place + width] = envelope[:, n * width : (n + 1) * width]


def on_device(loop, line, phases, tile_pairs, block_offsets, owners):
    freq_local, block_width, seg_count = phases.shape
    steps = loop // 2
    group = 2 if freq_local % 2 == 0 else 1
    halves = 2
    groups = freq_local // group
    units = steps * groups * halves
    part_rows = TILE * 2 * group // halves
    list_len = block_offsets.shape[1]
    both = 2 * seg_count
    gathered = pl.pallas_call(
        functools.partial(gather_kernel, loop, line, group, halves),
        out_shape=jax.ShapeDtypeStruct(
            (steps, line, groups, halves, part_rows, TILE), jnp.bfloat16
        ),
        in_specs=[pl.BlockSpec(memory_space=pltpu.HBM)] * 3,
        out_specs=pl.BlockSpec(memory_space=pl.ANY),
        scratch_shapes=[
            pltpu.SMEM(tile_pairs.shape, jnp.int32),
            pltpu.SMEM(block_offsets.shape, jnp.int32),
            pltpu.VMEM(phases.shape, jnp.float32),
            pltpu.VMEM((steps, 8, 128), jnp.int32),
            pltpu.VMEM((steps, 8, 128), jnp.int32),
            pltpu.VMEM((freq_local, block_width, both), jnp.bfloat16),
            pltpu.VMEM((steps, freq_local, TILE, both), jnp.bfloat16),
            pltpu.VMEM((steps, freq_local, TILE, both), jnp.bfloat16),
            pltpu.VMEM((TILE * 2 * group, TILE), jnp.float32),
            pltpu.VMEM((steps, groups, halves, part_rows, TILE), jnp.bfloat16),
            pltpu.SemaphoreType.DMA((2 + freq_local,)),
            pltpu.SemaphoreType.DMA((steps,)),
            pltpu.SemaphoreType.DMA((steps,)),
            pltpu.SemaphoreType.DMA((steps, freq_local)),
            pltpu.SemaphoreType.DMA((steps, freq_local)),
            pltpu.SemaphoreType.DMA((2, line - 1, units)),
            pltpu.SemaphoreType.DMA((2, line - 1, units)),
            pltpu.SemaphoreType.DMA((units,)),
        ],
        compiler_params=pltpu.CompilerParams(
            collective_id=0, has_side_effects=True, vmem_limit_bytes=58 * 2**20
        ),
        name="gather_products",
    )(tile_pairs, block_offsets, phases)

    rows = 32
    table = row_table(2 * group, SUBLANES // (2 * group))
    place = lax.axis_index("freq").astype(jnp.int32).reshape(1)

    def cross_block(slot, part, *refs):
        return slot_of(slot, *refs)[0], 0, part, 0

    return pl.pallas_call(
        functools.partial(lag_kernel, 1.0 / (F * seg_count)),
        out_shape=jax.ShapeDtypeStruct((CAP, LAGS, TILE * TILE), jnp.float32),
        grid_spec=pltpu.PrefetchScalarGridSpec(
            num_scalar_prefetch=3,
            grid=(CAP, TILE // rows),
            in_specs=[
                pl.BlockSpec(table.shape, lambda *_: (0, 0)),
                pl.BlockSpec((1, line * groups, rows * 2 * group, TILE), cross_block),
            ],
            out_specs=pl.BlockSpec(
                (1, LAGS, rows * TILE), lambda slot, part, *_: (slot, 0, part)
            ),
        ),
        compiler_params=pltpu.CompilerParams(vmem_limit_bytes=24 * 2**20),
        name="lag_sums",
    )(
        owners.reshape(list_len),
        block_offsets.reshape(list_len),
        place,
        jnp.asarray(table),
        gathered.reshape(steps, line * groups, TILE * 2 * group, TILE),
    )


def solution(mesh):
    in_specs = (
        P(("grp", "freq"), "chan", None),
        P("chan", None, None),
        P("chan", None),
        P("chan", None, None),
    )
    out_specs = P(("grp", "chan", "freq"), None, None)
    return jax.shard_map(
        functools.partial(on_device, mesh.shape["chan"], mesh.shape["freq"]),
        mesh=mesh,
        in_specs=in_specs,
        out_specs=out_specs,
        check_vma=False,
    )
```

```python
import functools
import math

import jax
import jax.numpy as jnp
import numpy as np
from jax import lax
from jax.experimental import pallas as pl
from jax.experimental.pallas import tpu as pltpu
from jax.sharding import PartitionSpec as P

F = 16
NFFT = 512
TILE = 128
CAP = 2
LAGS = 32
ROW_STEP = 32
SUBLANES = 16
ABREAST = 4
MESH = pl.DeviceIdType.MESH

SIN_TERMS = (
    0.999999999982969,
    -0.16666666616916945,
    0.008333330977498568,
    -0.00019840861553013607,
    2.752528712920731e-06,
    -2.3889498620743105e-08,
)
COS_TERMS = (
    0.99999999999925,
    -0.4999999999701845,
    0.04166666647312386,
    -0.0013888884175533636,
    2.4801040301795323e-05,
    -2.752468399134539e-07,
    1.9907690634373785e-09,
)


def polynomial(terms, u):
    total = jnp.full_like(u, terms[-1])
    for term in terms[-2::-1]:
        total = total * u + term
    return total


def cos_sin(x):
    half = x * 0.5
    u = half * half
    s = half * polynomial(SIN_TERMS, u)
    c = polynomial(COS_TERMS, u)
    twice = s + s
    return 1.0 - twice * s, twice * c


def lag_table():
    bins = np.arange(F, dtype=np.float64) + 32.0
    lag_index = np.arange(LAGS, dtype=np.float64) - float(LAGS // 2)
    angles = 2.0 * math.pi / NFFT * bins[:, None] * lag_index[None, :]
    cosine, sine = np.cos(angles), np.sin(angles)
    real_rows = np.concatenate([cosine, sine], axis=1)
    imag_rows = np.concatenate([-sine, cosine], axis=1)
    return np.stack([real_rows, imag_rows], axis=1).reshape(2 * F, 2 * LAGS)


def row_table(parts, rows):
    table = lag_table().reshape(2 * F // parts, parts, 2 * LAGS)
    spread = np.einsum("ab,ukl->alubk", np.eye(rows), table)
    spread = spread.reshape(rows * 2 * LAGS, 2 * F * rows)
    high = spread.astype(np.float32).astype(jnp.bfloat16)
    low = (spread - high.astype(np.float64)).astype(np.float32).astype(jnp.bfloat16)
    return np.concatenate([high, low], axis=1)


def gather_kernel(
    loop,
    line,
    group,
    halves,
    pairs_hbm,
    offsets_hbm,
    phases_hbm,
    all_ref,
    pairs_ref,
    offsets_ref,
    phases_ref,
    want,
    asked,
    spec,
    going,
    coming,
    mixed,
    own,
    in_sem,
    want_send,
    want_recv,
    tile_send,
    tile_recv,
    line_send,
    line_recv,
    local_sem,
):
    me = lax.axis_index("chan")
    pos = lax.axis_index("freq")
    freq_local, block_width, seg_count = phases_ref.shape
    steps = want.shape[0]
    list_len = offsets_ref.shape[1]

    sources = [(pairs_hbm, pairs_ref), (offsets_hbm, offsets_ref)]
    sources += [(phases_hbm.at[f], phases_ref.at[f]) for f in range(freq_local)]
    fetched = [
        pltpu.make_async_copy(source, target, in_sem.at[n])
        for n, (source, target) in enumerate(sources)
    ]
    for copy in fetched:
        copy.start()

    def at_chan(delta):
        return {"chan": lax.rem(me + (delta % loop), loop)}

    def at_freq(delta):
        return {"freq": lax.rem(pos + (delta % line), line)}

    chan_deltas = sorted(
        {(sign * (o + 1)) % loop for o in range(steps) for sign in (1, -1)} - {0}
    )
    freq_deltas = sorted({1 % line, -1 % line} - {0})
    barrier = pltpu.get_barrier_semaphore()
    for delta in chan_deltas:
        pl.semaphore_signal(barrier, inc=1, device_id=at_chan(delta), device_id_type=MESH)
    for delta in freq_deltas:
        pl.semaphore_signal(barrier, inc=1, device_id=at_freq(delta), device_id_type=MESH)
    pl.semaphore_wait(barrier, len(chan_deltas) + len(freq_deltas))

    fetched[0].wait()
    fetched[1].wait()

    left_tiles = []
    want_copies = []
    for o in range(steps):
        row_tile = jnp.int32(0)
        col_tile = jnp.int32(0)
        for e in range(list_len):
            here = offsets_ref[0, e] == o
            row_tile = row_tile + jnp.where(here, pairs_ref[0, e, 0], 0)
            col_tile = col_tile + jnp.where(here, pairs_ref[0, e, 1], 0)
        left_tiles.append(row_tile)
        want[o] = jnp.full(want.shape[1:], col_tile, jnp.int32)
        copy = pltpu.make_async_remote_copy(
            src_ref=want.at[o],
            dst_ref=asked.at[o],
            send_sem=want_send.at[o],
            recv_sem=want_recv.at[o],
            device_id=at_chan(o + 1),
            device_id_type=MESH,
        )
        copy.start()
        want_copies.append(copy)

    def tile_of(f, index):
        chosen = spec[f, 0:TILE, :]
        for t in range(1, block_width // TILE):
            chosen = jnp.where(index == t, spec[f, t * TILE : (t + 1) * TILE, :], chosen)
        return chosen

    tile_copies = {}
    asked_tiles = {}

    def make_spectra(f):
        fetched[2 + f].wait()

        @pl.loop(0, block_width // ROW_STEP)
        def _(step):
            rows = pl.ds(pl.multiple_of(step * ROW_STEP, ROW_STEP), ROW_STEP)
            c, s = cos_sin(phases_ref[f, rows, :])
            spec[f, rows, 0:seg_count] = c.astype(jnp.bfloat16)
            spec[f, rows, seg_count:] = s.astype(jnp.bfloat16)

    def send_tile(o, f):
        if o not in asked_tiles:
            want_copies[o].wait_recv()
            asked_tiles[o] = jnp.max(asked[o])
        going[o, f] = tile_of(f, asked_tiles[o])
        copy = pltpu.make_async_remote_copy(
            src_ref=going.at[o, f],
            dst_ref=coming.at[o, f],
            send_sem=tile_send.at[o, f],
            recv_sem=tile_recv.at[o, f],
            device_id=at_chan(-(o + 1)),
            device_id_type=MESH,
        )
        copy.start()
        tile_copies[o, f] = copy

    pieces = [(o, g) for g in range(freq_local // group) for o in range(steps)]

    def send_piece(number):
        if number < len(pieces):
            o, g = pieces[number]
            for f in range(g * group, (g + 1) * group):
                send_tile(o, f)

    for f in range(group):
        make_spectra(f)
        send_tile(0, f)
    for f in range(group, freq_local):
        make_spectra(f)

    units = [
        (o, g, h)
        for g in range(freq_local // group)
        for o in range(steps)
        for h in range(halves)
    ]
    part_rows = TILE * 2 * group // halves

    def line_copy(right, stage, unit, origin, source=None):
        o, g, h = units[unit]
        place = all_ref.at[o, origin, g, h]
        way = 0 if right else 1
        return pltpu.make_async_remote_copy(
            src_ref=place if source is None else source,
            dst_ref=place,
            send_sem=line_send.at[way, stage, unit],
            recv_sem=line_recv.at[way, stage, unit],
            device_id=at_freq(1 if right else -1),
            device_id_type=MESH,
        )

    def can_send(right):
        return pos < line - 1 if right else pos > 0

    def arrives(right, stage):
        return pos - (stage + 1) >= 0 if right else pos + (stage + 1) <= line - 1

    def origin_at(right, stage):
        return pos - stage if right else pos + stage

    def take_and_forward(stage, unit):
        for right in (True, False):

            @pl.when(arrives(right, stage))
            def _():
                origin = origin_at(right, stage + 1)
                line_copy(right, stage, unit, origin).wait_recv()
                if stage + 1 < line - 1:

                    @pl.when(can_send(right))
                    def _():
                        line_copy(right, stage + 1, unit, origin).start()

    local_copies = []
    for turn in range(len(units) + line - 1):
        if turn < len(units):
            o, g, h = units[turn]
            if h == 0:
                for n in range(group):
                    tile_copies[o, g * group + n].wait_recv()
                send_piece(turn // halves + 1)
                for n in range(group):
                    f = g * group + n
                    left = tile_of(f, left_tiles[o])
                    swapped = jnp.concatenate(
                        [left[:, seg_count:], -left[:, :seg_count]], axis=1
                    )
                    products = lax.dot_general(
                        jnp.concatenate([left, swapped], axis=0),
                        coming[o, f],
                        (((1,), (1,)), ((), ())),
                        preferred_element_type=jnp.float32,
                    )
                    stride = 2 * group
                    mixed[pl.ds(2 * n, TILE, stride=stride), :] = products[:TILE]
                    mixed[pl.ds(2 * n + 1, TILE, stride=stride), :] = products[TILE:]
            own[o, g, h] = mixed[h * part_rows : (h + 1) * part_rows, :].astype(own.dtype)
            for right in (True, False):

                @pl.when(can_send(right))
                def _():
                    line_copy(right, 0, turn, pos, own.at[o, g, h]).start()

            copy = pltpu.make_async_copy(
                own.at[o, g, h], all_ref.at[o, pos, g, h], local_sem.at[turn]
            )
            copy.start()
            local_copies.append(copy)
        for stage in range(line - 1):
            unit = turn - 1 - stage
            if 0 <= unit < len(units):
                take_and_forward(stage, unit)

    for copy in local_copies:
        copy.wait()
    for copy in want_copies:
        copy.wait_send()
    for copy in tile_copies.values():
        copy.wait_send()
    for unit, (o, g, h) in enumerate(units):
        for right in (True, False):

            @pl.when(can_send(right))
            def _():
                line_copy(right, 0, unit, pos, own.at[o, g, h]).wait_send()
                for stage in range(line - 2):

                    @pl.when(arrives(right, stage))
                    def _():
                        origin = origin_at(right, stage + 1)
                        line_copy(right, stage + 1, unit, origin).wait_send()


def slot_of(slot, owners_ref, offsets_ref, place_ref):
    earlier, chosen, found = jnp.int32(0), jnp.int32(0), jnp.int32(0)
    for e in range(offsets_ref.shape[0]):
        mine = owners_ref[e] == place_ref[0]
        hit = jnp.logical_and(mine, earlier == slot)
        chosen = jnp.where(hit, offsets_ref[e], chosen)
        found = jnp.where(hit, 1, found)
        earlier = earlier + jnp.where(mine, 1, 0)
    return chosen, found


def lag_kernel(
    env_scale, owners_ref, offsets_ref, place_ref, table_ref, cross_ref, out_ref
):
    _, groups, block_rows, width = cross_ref.shape
    _, found = slot_of(pl.program_id(0), owners_ref, offsets_ref, place_ref)
    scale = jnp.where(found == 1, jnp.float32(env_scale), jnp.float32(0.0))
    table = table_ref[...]
    rows_at_once = table.shape[0] // (2 * LAGS)

    def stacked(at):
        start = at * SUBLANES
        return jnp.concatenate(
            [cross_ref[0, u, start : start + SUBLANES, :] for u in range(groups)], axis=0
        )

    for at in range(0, block_rows // SUBLANES, ABREAST):
        beside = jnp.concatenate([stacked(at + n) for n in range(ABREAST)], axis=1)
        lagged = jnp.dot(
            table,
            jnp.concatenate([beside, beside], axis=0),
            preferred_element_type=jnp.float32,
        )
        for i in range(rows_at_once):
            start = i * 2 * LAGS
            real = lagged[start : start + LAGS]
            imag = lagged[start + LAGS : start + 2 * LAGS]
            envelope = (real * real + imag * imag) * scale
            for n in range(ABREAST):
                place = ((at + n) * rows_at_once + i) * width
                out_ref[0, :, place : place + width] = envelope[:, n * width : (n + 1) * width]


def on_device(loop, line, phases, tile_pairs, block_offsets, owners):
    freq_local, block_width, seg_count = phases.shape
    steps = loop // 2
    group = 2 if freq_local % 2 == 0 else 1
    halves = 2
    groups = freq_local // group
    units = steps * groups * halves
    part_rows = TILE * 2 * group // halves
    list_len = block_offsets.shape[1]
    both = 2 * seg_count
    gathered = pl.pallas_call(
        functools.partial(gather_kernel, loop, line, group, halves),
        out_shape=jax.ShapeDtypeStruct(
            (steps, line, groups, halves, part_rows, TILE), jnp.bfloat16
        ),
        in_specs=[pl.BlockSpec(memory_space=pltpu.HBM)] * 3,
        out_specs=pl.BlockSpec(memory_space=pl.ANY),
        scratch_shapes=[
            pltpu.SMEM(tile_pairs.shape, jnp.int32),
            pltpu.SMEM(block_offsets.shape, jnp.int32),
            pltpu.VMEM(phases.shape, jnp.float32),
            pltpu.VMEM((steps, 8, 128), jnp.int32),
            pltpu.VMEM((steps, 8, 128), jnp.int32),
            pltpu.VMEM((freq_local, block_width, both), jnp.bfloat16),
            pltpu.VMEM((steps, freq_local, TILE, both), jnp.bfloat16),
            pltpu.VMEM((steps, freq_local, TILE, both), jnp.bfloat16),
            pltpu.VMEM((TILE * 2 * group, TILE), jnp.float32),
            pltpu.VMEM((steps, groups, halves, part_rows, TILE), jnp.bfloat16),
            pltpu.SemaphoreType.DMA((2 + freq_local,)),
            pltpu.SemaphoreType.DMA((steps,)),
            pltpu.SemaphoreType.DMA((steps,)),
            pltpu.SemaphoreType.DMA((steps, freq_local)),
            pltpu.SemaphoreType.DMA((steps, freq_local)),
            pltpu.SemaphoreType.DMA((2, line - 1, units)),
            pltpu.SemaphoreType.DMA((2, line - 1, units)),
            pltpu.SemaphoreType.DMA((units,)),
        ],
        compiler_params=pltpu.CompilerParams(
            collective_id=0, has_side_effects=True, vmem_limit_bytes=58 * 2**20
        ),
        name="gather_products",
    )(tile_pairs, block_offsets, phases)

    rows = 32
    table = row_table(2 * group, SUBLANES // (2 * group))
    place = lax.axis_index("freq").astype(jnp.int32).reshape(1)

    def cross_block(slot, part, *refs):
        return slot_of(slot, *refs)[0], 0, part, 0

    return pl.pallas_call(
        functools.partial(lag_kernel, 1.0 / (F * seg_count)),
        out_shape=jax.ShapeDtypeStruct((CAP, LAGS, TILE * TILE), jnp.float32),
        grid_spec=pltpu.PrefetchScalarGridSpec(
            num_scalar_prefetch=3,
            grid=(CAP, TILE // rows),
            in_specs=[
                pl.BlockSpec(table.shape, lambda *_: (0, 0)),
                pl.BlockSpec((1, line * groups, rows * 2 * group, TILE), cross_block),
            ],
            out_specs=pl.BlockSpec(
                (1, LAGS, rows * TILE), lambda slot, part, *_: (slot, 0, part)
            ),
        ),
        compiler_params=pltpu.CompilerParams(vmem_limit_bytes=58 * 2**20),
        name="lag_sums",
    )(
        owners.reshape(list_len),
        block_offsets.reshape(list_len),
        place,
        jnp.asarray(table),
        gathered.reshape(steps, line * groups, TILE * 2 * group, TILE),
    )


def solution(mesh):
    in_specs = (
        P(("grp", "freq"), "chan", None),
        P("chan", None, None),
        P("chan", None),
        P("chan", None, None),
    )
    out_specs = P(("grp", "chan", "freq"), None, None)
    return jax.shard_map(
        functools.partial(on_device, mesh.shape["chan"], mesh.shape["freq"]),
        mesh=mesh,
        in_specs=in_specs,
        out_specs=out_specs,
        check_vma=False,
    )
```

```python
import functools
import math

import jax
import jax.numpy as jnp
import numpy as np
from jax import lax
from jax.experimental import pallas as pl
from jax.experimental.pallas import tpu as pltpu
from jax.sharding import PartitionSpec as P

F = 16
NFFT = 512
TILE = 128
CAP = 2
LAGS = 32
ROW_STEP = 32
SUBLANES = 16
ABREAST = 2
MESH = pl.DeviceIdType.MESH

SIN_TERMS = (
    0.999999999982969,
    -0.16666666616916945,
    0.008333330977498568,
    -0.00019840861553013607,
    2.752528712920731e-06,
    -2.3889498620743105e-08,
)
COS_TERMS = (
    0.99999999999925,
    -0.4999999999701845,
    0.04166666647312386,
    -0.0013888884175533636,
    2.4801040301795323e-05,
    -2.752468399134539e-07,
    1.9907690634373785e-09,
)


def polynomial(terms, u):
    total = jnp.full_like(u, terms[-1])
    for term in terms[-2::-1]:
        total = total * u + term
    return total


def cos_sin(x):
    half = x * 0.5
    u = half * half
    s = half * polynomial(SIN_TERMS, u)
    c = polynomial(COS_TERMS, u)
    twice = s + s
    return 1.0 - twice * s, twice * c


def lag_table():
    bins = np.arange(F, dtype=np.float64) + 32.0
    lag_index = np.arange(LAGS, dtype=np.float64) - float(LAGS // 2)
    angles = 2.0 * math.pi / NFFT * bins[:, None] * lag_index[None, :]
    cosine, sine = np.cos(angles), np.sin(angles)
    real_rows = np.concatenate([cosine, sine], axis=1)
    imag_rows = np.concatenate([-sine, cosine], axis=1)
    return np.stack([real_rows, imag_rows], axis=1).reshape(2 * F, 2 * LAGS)


def row_table(parts, rows):
    table = lag_table().reshape(2 * F // parts, parts, 2 * LAGS)
    spread = np.einsum("ab,ukl->alubk", np.eye(rows), table)
    spread = spread.reshape(rows * 2 * LAGS, 2 * F * rows)
    high = spread.astype(np.float32).astype(jnp.bfloat16)
    low = (spread - high.astype(np.float64)).astype(np.float32).astype(jnp.bfloat16)
    return np.concatenate([high, low], axis=1)


def gather_kernel(
    loop,
    line,
    group,
    halves,
    pairs_hbm,
    offsets_hbm,
    phases_hbm,
    all_ref,
    pairs_ref,
    offsets_ref,
    phases_ref,
    want,
    asked,
    spec,
    going,
    coming,
    mixed,
    own,
    in_sem,
    want_send,
    want_recv,
    tile_send,
    tile_recv,
    line_send,
    line_recv,
    local_sem,
):
    me = lax.axis_index("chan")
    pos = lax.axis_index("freq")
    freq_local, block_width, seg_count = phases_ref.shape
    steps = want.shape[0]
    list_len = offsets_ref.shape[1]

    sources = [(pairs_hbm, pairs_ref), (offsets_hbm, offsets_ref)]
    sources += [(phases_hbm.at[f], phases_ref.at[f]) for f in range(freq_local)]
    fetched = [
        pltpu.make_async_copy(source, target, in_sem.at[n])
        for n, (source, target) in enumerate(sources)
    ]
    for copy in fetched:
        copy.start()

    def at_chan(delta):
        return {"chan": lax.rem(me + (delta % loop), loop)}

    def at_freq(delta):
        return {"freq": lax.rem(pos + (delta % line), line)}

    chan_deltas = sorted(
        {(sign * (o + 1)) % loop for o in range(steps) for sign in (1, -1)} - {0}
    )
    freq_deltas = sorted({1 % line, -1 % line} - {0})
    barrier = pltpu.get_barrier_semaphore()
    for delta in chan_deltas:
        pl.semaphore_signal(barrier, inc=1, device_id=at_chan(delta), device_id_type=MESH)
    for delta in freq_deltas:
        pl.semaphore_signal(barrier, inc=1, device_id=at_freq(delta), device_id_type=MESH)
    pl.semaphore_wait(barrier, len(chan_deltas) + len(freq_deltas))

    fetched[0].wait()
    fetched[1].wait()

    left_tiles = []
    want_copies = []
    for o in range(steps):
        row_tile = jnp.int32(0)
        col_tile = jnp.int32(0)
        for e in range(list_len):
            here = offsets_ref[0, e] == o
            row_tile = row_tile + jnp.where(here, pairs_ref[0, e, 0], 0)
            col_tile = col_tile + jnp.where(here, pairs_ref[0, e, 1], 0)
        left_tiles.append(row_tile)
        want[o] = jnp.full(want.shape[1:], col_tile, jnp.int32)
        copy = pltpu.make_async_remote_copy(
            src_ref=want.at[o],
            dst_ref=asked.at[o],
            send_sem=want_send.at[o],
            recv_sem=want_recv.at[o],
            device_id=at_chan(o + 1),
            device_id_type=MESH,
        )
        copy.start()
        want_copies.append(copy)

    def tile_of(f, index):
        chosen = spec[f, 0:TILE, :]
        for t in range(1, block_width // TILE):
            chosen = jnp.where(index == t, spec[f, t * TILE : (t + 1) * TILE, :], chosen)
        return chosen

    tile_copies = {}
    asked_tiles = {}

    def make_spectra(f):
        fetched[2 + f].wait()

        @pl.loop(0, block_width // ROW_STEP)
        def _(step):
            rows = pl.ds(pl.multiple_of(step * ROW_STEP, ROW_STEP), ROW_STEP)
            c, s = cos_sin(phases_ref[f, rows, :])
            spec[f, rows, 0:seg_count] = c.astype(jnp.bfloat16)
            spec[f, rows, seg_count:] = s.astype(jnp.bfloat16)

    def send_tile(o, f):
        if o not in asked_tiles:
            want_copies[o].wait_recv()
            asked_tiles[o] = jnp.max(asked[o])
        going[o, f] = tile_of(f, asked_tiles[o])
        copy = pltpu.make_async_remote_copy(
            src_ref=going.at[o, f],
            dst_ref=coming.at[o, f],
            send_sem=tile_send.at[o, f],
            recv_sem=tile_recv.at[o, f],
            device_id=at_chan(-(o + 1)),
            device_id_type=MESH,
        )
        copy.start()
        tile_copies[o, f] = copy

    pieces = [(o, g) for g in range(freq_local // group) for o in range(steps)]

    def send_piece(number):
        if number < len(pieces):
            o, g = pieces[number]
            for f in range(g * group, (g + 1) * group):
                send_tile(o, f)

    for f in range(group):
        make_spectra(f)
        send_tile(0, f)
    for f in range(group, freq_local):
        make_spectra(f)

    units = [
        (o, g, h)
        for g in range(freq_local // group)
        for o in range(steps)
        for h in range(halves)
    ]
    part_rows = TILE * 2 * group // halves

    def line_copy(right, stage, unit, origin, source=None):
        o, g, h = units[unit]
        place = all_ref.at[o, origin, g, h]
        way = 0 if right else 1
        return pltpu.make_async_remote_copy(
            src_ref=place if source is None else source,
            dst_ref=place,
            send_sem=line_send.at[way, stage, unit],
            recv_sem=line_recv.at[way, stage, unit],
            device_id=at_freq(1 if right else -1),
            device_id_type=MESH,
        )

    def can_send(right):
        return pos < line - 1 if right else pos > 0

    def arrives(right, stage):
        return pos - (stage + 1) >= 0 if right else pos + (stage + 1) <= line - 1

    def origin_at(right, stage):
        return pos - stage if right else pos + stage

    def take_and_forward(stage, unit):
        for right in (True, False):

            @pl.when(arrives(right, stage))
            def _():
                origin = origin_at(right, stage + 1)
                line_copy(right, stage, unit, origin).wait_recv()
                if stage + 1 < line - 1:

                    @pl.when(can_send(right))
                    def _():
                        line_copy(right, stage + 1, unit, origin).start()

    local_copies = []
    for turn in range(len(units) + line - 1):
        if turn < len(units):
            o, g, h = units[turn]
            if h == 0:
                for n in range(group):
                    tile_copies[o, g * group + n].wait_recv()
                send_piece(turn // halves + 1)
                for n in range(group):
                    f = g * group + n
                    left = tile_of(f, left_tiles[o])
                    swapped = jnp.concatenate(
                        [left[:, seg_count:], -left[:, :seg_count]], axis=1
                    )
                    products = lax.dot_general(
                        jnp.concatenate([left, swapped], axis=0),
                        coming[o, f],
                        (((1,), (1,)), ((), ())),
                        preferred_element_type=jnp.float32,
                    )
                    stride = 2 * group
                    mixed[pl.ds(2 * n, TILE, stride=stride), :] = products[:TILE]
                    mixed[pl.ds(2 * n + 1, TILE, stride=stride), :] = products[TILE:]
            own[o, g, h] = mixed[h * part_rows : (h + 1) * part_rows, :].astype(own.dtype)
            for right in (True, False):

                @pl.when(can_send(right))
                def _():
                    line_copy(right, 0, turn, pos, own.at[o, g, h]).start()

            copy = pltpu.make_async_copy(
                own.at[o, g, h], all_ref.at[o, pos, g, h], local_sem.at[turn]
            )
            copy.start()
            local_copies.append(copy)
        for stage in range(line - 1):
            unit = turn - 1 - stage
            if 0 <= unit < len(units):
                take_and_forward(stage, unit)

    for copy in local_copies:
        copy.wait()
    for copy in want_copies:
        copy.wait_send()
    for copy in tile_copies.values():
        copy.wait_send()
    for unit, (o, g, h) in enumerate(units):
        for right in (True, False):

            @pl.when(can_send(right))
            def _():
                line_copy(right, 0, unit, pos, own.at[o, g, h]).wait_send()
                for stage in range(line - 2):

                    @pl.when(arrives(right, stage))
                    def _():
                        origin = origin_at(right, stage + 1)
                        line_copy(right, stage + 1, unit, origin).wait_send()


def slot_of(slot, owners_ref, offsets_ref, place_ref):
    earlier, chosen, found = jnp.int32(0), jnp.int32(0), jnp.int32(0)
    for e in range(offsets_ref.shape[0]):
        mine = owners_ref[e] == place_ref[0]
        hit = jnp.logical_and(mine, earlier == slot)
        chosen = jnp.where(hit, offsets_ref[e], chosen)
        found = jnp.where(hit, 1, found)
        earlier = earlier + jnp.where(mine, 1, 0)
    return chosen, found


def lag_kernel(
    env_scale, owners_ref, offsets_ref, place_ref, table_ref, cross_ref, out_ref
):
    _, groups, block_rows, width = cross_ref.shape
    _, found = slot_of(pl.program_id(0), owners_ref, offsets_ref, place_ref)
    scale = jnp.where(found == 1, jnp.float32(env_scale), jnp.float32(0.0))
    table = table_ref[...]
    rows_at_once = table.shape[0] // (2 * LAGS)

    def stacked(at):
        start = at * SUBLANES
        return jnp.concatenate(
            [cross_ref[0, u, start : start + SUBLANES, :] for u in range(groups)], axis=0
        )

    for at in range(0, block_rows // SUBLANES, ABREAST):
        beside = jnp.concatenate([stacked(at + n) for n in range(ABREAST)], axis=1)
        lagged = jnp.dot(
            table,
            jnp.concatenate([beside, beside], axis=0),
            preferred_element_type=jnp.float32,
        )
        for i in range(rows_at_once):
            start = i * 2 * LAGS
            real = lagged[start : start + LAGS]
            imag = lagged[start + LAGS : start + 2 * LAGS]
            envelope = (real * real + imag * imag) * scale
            for n in range(ABREAST):
                place = ((at + n) * rows_at_once + i) * width
                out_ref[0, :, place : place + width] = envelope[:, n * width : (n + 1) * width]


def on_device(loop, line, phases, tile_pairs, block_offsets, owners):
    freq_local, block_width, seg_count = phases.shape
    steps = loop // 2
    group = 2 if freq_local % 2 == 0 else 1
    halves = 2
    groups = freq_local // group
    units = steps * groups * halves
    part_rows = TILE * 2 * group // halves
    list_len = block_offsets.shape[1]
    both = 2 * seg_count
    gathered = pl.pallas_call(
        functools.partial(gather_kernel, loop, line, group, halves),
        out_shape=jax.ShapeDtypeStruct(
            (steps, line, groups, halves, part_rows, TILE), jnp.bfloat16
        ),
        in_specs=[pl.BlockSpec(memory_space=pltpu.HBM)] * 3,
        out_specs=pl.BlockSpec(memory_space=pl.ANY),
        scratch_shapes=[
            pltpu.SMEM(tile_pairs.shape, jnp.int32),
            pltpu.SMEM(block_offsets.shape, jnp.int32),
            pltpu.VMEM(phases.shape, jnp.float32),
            pltpu.VMEM((steps, 8, 128), jnp.int32),
            pltpu.VMEM((steps, 8, 128), jnp.int32),
            pltpu.VMEM((freq_local, block_width, both), jnp.bfloat16),
            pltpu.VMEM((steps, freq_local, TILE, both), jnp.bfloat16),
            pltpu.VMEM((steps, freq_local, TILE, both), jnp.bfloat16),
            pltpu.VMEM((TILE * 2 * group, TILE), jnp.float32),
            pltpu.VMEM((steps, groups, halves, part_rows, TILE), jnp.bfloat16),
            pltpu.SemaphoreType.DMA((2 + freq_local,)),
            pltpu.SemaphoreType.DMA((steps,)),
            pltpu.SemaphoreType.DMA((steps,)),
            pltpu.SemaphoreType.DMA((steps, freq_local)),
            pltpu.SemaphoreType.DMA((steps, freq_local)),
            pltpu.SemaphoreType.DMA((2, line - 1, units)),
            pltpu.SemaphoreType.DMA((2, line - 1, units)),
            pltpu.SemaphoreType.DMA((units,)),
        ],
        compiler_params=pltpu.CompilerParams(
            collective_id=0, has_side_effects=True, vmem_limit_bytes=58 * 2**20
        ),
        name="gather_products",
    )(tile_pairs, block_offsets, phases)

    rows = 128
    table = row_table(2 * group, SUBLANES // (2 * group))
    place = lax.axis_index("freq").astype(jnp.int32).reshape(1)

    def cross_block(slot, part, *refs):
        return slot_of(slot, *refs)[0], 0, part, 0

    return pl.pallas_call(
        functools.partial(lag_kernel, 1.0 / (F * seg_count)),
        out_shape=jax.ShapeDtypeStruct((CAP, LAGS, TILE * TILE), jnp.float32),
        grid_spec=pltpu.PrefetchScalarGridSpec(
            num_scalar_prefetch=3,
            grid=(CAP, TILE // rows),
            in_specs=[
                pl.BlockSpec(table.shape, lambda *_: (0, 0)),
                pl.BlockSpec((1, line * groups, rows * 2 * group, TILE), cross_block),
            ],
            out_specs=pl.BlockSpec(
                (1, LAGS, rows * TILE), lambda slot, part, *_: (slot, 0, part)
            ),
        ),
        compiler_params=pltpu.CompilerParams(vmem_limit_bytes=58 * 2**20),
        name="lag_sums",
    )(
        owners.reshape(list_len),
        block_offsets.reshape(list_len),
        place,
        jnp.asarray(table),
        gathered.reshape(steps, line * groups, TILE * 2 * group, TILE),
    )


def solution(mesh):
    in_specs = (
        P(("grp", "freq"), "chan", None),
        P("chan", None, None),
        P("chan", None),
        P("chan", None, None),
    )
    out_specs = P(("grp", "chan", "freq"), None, None)
    return jax.shard_map(
        functools.partial(on_device, mesh.shape["chan"], mesh.shape["freq"]),
        mesh=mesh,
        in_specs=in_specs,
        out_specs=out_specs,
        check_vma=False,
    )
```
